32 devices in a mesh: grp: 2 (over x), row: 8 (over z, y), col: 2 (over core).
Axes of the slice: x: 2, y: 2, z: 4, core: 2. Of those that a mesh axis runs over, the one named last changes fastest.
Arguments:
- pair_grid: bfloat16 [256, 128, 128], P(('grp', 'row'), 'col'), parts along dimension 0, may hold values from -6 to 6
- token_mask: int32 [256], P('grp'), parts along dimension 0, may hold values 0 or 1
- proj_weight: bfloat16 [128, 512], replicated, may hold values from -0.5 to 0.5
- gate_weight: bfloat16 [128, 128], replicated, may hold values from -0.5 to 0.5
- out_weight: bfloat16 [128, 128], replicated, may hold values from -0.5 to 0.5
- in_gain: float32 [128], replicated, may hold values from 0.5 to 1.5
- out_gain: float32 [128], replicated, may hold values from 0.5 to 1.5
Outputs:
- update: bfloat16 [256, 128, 128], P(('grp', 'row'), 'col'), parts along dimension 0
The draws below stay inside these ranges and needn't reach their ends.
There are 2 independent parts, one for each index of `grp`. The reference program is written for one: setup_inputs(seed, part) draws one part's arguments, and reference() takes and returns one part's arrays. A program takes and returns all parts, laid end to end along the dimension named above; an argument that names none is the same for every part. Nothing has to cross between parts.
All inputs are finite; a program needn't handle non-finite values.
Results may differ from the reference program's by a relative error of at most 0.0079.
Values may be sent and summed in bfloat16 or wider, within the bound.
A program may use at most 128 MiB of HBM per device.

```python
import jax
import jax.numpy as jnp
from jax import lax

C = 128
TOKENS = 128


def with_ends(array, rng, least, top_value):
    longest = array.shape.index(max(array.shape))
    spots = []
    for shift in (0, 1):
        where = [jax.random.randint(jax.random.fold_in(rng, axis), (), 0, length) for axis, length in enumerate(array.shape)]
        where[longest] = (where[longest] + shift) % array.shape[longest]
        spots.append(tuple(where))
    return array.at[spots[0]].set(least).at[spots[1]].set(top_value)


def level_of(stream_key, extent, cuts, low, top_value):
    level, own = 1.0, jax.random.fold_in(stream_key, 6)
    for axis_at, shards_of in cuts:
        heights = jnp.exp(jax.random.uniform(jax.random.fold_in(own, axis_at), (shards_of,), jnp.float32, low / len(cuts), top_value / len(cuts)))
        level = level * jnp.repeat(heights, extent[axis_at] // shards_of).reshape([-1 if axis == axis_at else 1 for axis in range(len(extent))])
    return level


def noise(stream_key, shape, deviation, bound, split=(), kind=jnp.bfloat16):
    level = level_of(stream_key, shape, split, -0.22, 0.18) if split else 1.0
    drawn = jax.random.normal(stream_key, shape, jnp.float32) * deviation * level
    return jnp.minimum(jnp.maximum(drawn, -bound), bound).astype(kind)


def setup_inputs(seed: int = 0, part: int = 0) -> dict:
    splits = jax.random.split(jax.random.key(seed), 8)
    part_keys = jax.random.split(jax.random.fold_in(splits[7], part), 8)
    return {
        "pair_grid": noise(part_keys[0], (TOKENS, TOKENS, C), 1.0, 6.0, ((0, 8), (1, 2))),
        "token_mask": with_ends((jax.random.randint(part_keys[1], (TOKENS,), 0, 8) < 7).astype(jnp.int32), jax.random.fold_in(part_keys[1], 1), 0, 1),
        "proj_weight": noise(splits[2], (C, 4 * C), C ** -0.5, 0.5),
        "gate_weight": noise(splits[3], (C, C), C ** -0.5, 0.5),
        "out_weight": noise(splits[4], (C, C), C ** -0.5, 0.5),
        "in_gain": jnp.clip(jax.random.uniform(splits[5], (C,), jnp.float32, 0.5, 1.5), 0.5, 1.5),
        "out_gain": jnp.clip(jax.random.uniform(splits[6], (C,), jnp.float32, 0.5, 1.5), 0.5, 1.5),
    }


def layer_norm(inputs, scales, along):
    centre = lax.optimization_barrier(jnp.mean(inputs, axis=along, keepdims=True))
    shifted = inputs - centre
    spread = lax.optimization_barrier(jnp.mean(shifted * shifted, axis=along, keepdims=True))
    return shifted * lax.rsqrt(spread + 1e-05) * scales

def reference(pair_grid, token_mask, proj_weight, gate_weight, out_weight, in_gain, out_gain):
    channels = pair_grid.shape[-1]
    normed = layer_norm(pair_grid.astype(jnp.float32), in_gain, -1).astype(jnp.bfloat16)
    flat_cells = normed.reshape(-1, channels)
    projected = jnp.dot(flat_cells, proj_weight, preferred_element_type=jnp.float32).reshape(TOKENS, TOKENS, 4 * channels)
    valid = token_mask.astype(jnp.float32)
    pair_mask = (valid[:, None] * valid[None, :])[..., None]
    left_side = (pair_mask * jax.nn.sigmoid(projected[..., :channels]) * projected[..., channels:2 * channels]).astype(jnp.bfloat16)
    right_side = (pair_mask * jax.nn.sigmoid(projected[..., 2 * channels:3 * channels]) * projected[..., 3 * channels:]).astype(jnp.bfloat16)
    out_gate = jax.nn.sigmoid(jnp.dot(flat_cells, gate_weight, preferred_element_type=jnp.float32)).reshape(TOKENS, TOKENS, channels)
    combined = jnp.einsum('ikc,jkc->ijc', left_side.astype(jnp.float32), right_side.astype(jnp.float32), precision=lax.Precision.HIGHEST)
    normed_out = layer_norm(combined, out_gain, -1).astype(jnp.bfloat16)
    update = out_gate * jnp.dot(normed_out.reshape(-1, channels), out_weight, preferred_element_type=jnp.float32).reshape(TOKENS, TOKENS, channels)
    return update.astype(jnp.bfloat16)
```

```python
import jax
import jax.numpy as jnp
from jax import lax
from jax.experimental import pallas as pl
from jax.experimental.pallas import tpu as pltpu
from jax.sharding import PartitionSpec as P

MESH = pl.DeviceIdType.MESH
F32 = jnp.float32
BF16 = jnp.bfloat16
NY = 2
PIECES = 2
HALF = 8


def layer_norm(inputs, scales, along):
    centre = jnp.mean(inputs, axis=along, keepdims=True)
    shifted = inputs - centre
    spread = jnp.mean(shifted * shifted, axis=along, keepdims=True)
    return shifted * lax.rsqrt(spread + 1e-05) * scales


def body(pair_grid, token_mask, proj_weight, gate_weight, out_weight, in_gain, out_gain):
    row_count, col_count, channels = pair_grid.shape
    row_offset = lax.axis_index("row") * row_count
    col_offset = lax.axis_index("col") * col_count
    row_valid = lax.dynamic_slice_in_dim(token_mask, row_offset, row_count).astype(jnp.float32)
    col_valid = lax.dynamic_slice_in_dim(token_mask, col_offset, col_count).astype(jnp.float32)
    normed = layer_norm(pair_grid.astype(jnp.float32), in_gain, -1).astype(jnp.bfloat16)
    flat_cells = normed.reshape(-1, channels)
    projected = jnp.dot(flat_cells, proj_weight, preferred_element_type=jnp.float32).reshape(
        row_count, col_count, 4 * channels
    )
    pair_mask = (row_valid[:, None] * col_valid[None, :])[..., None]
    left_side = (
        pair_mask
        * jax.nn.sigmoid(projected[..., :channels])
        * projected[..., channels : 2 * channels]
    ).astype(jnp.bfloat16)
    right_side = (
        pair_mask
        * jax.nn.sigmoid(projected[..., 2 * channels : 3 * channels])
        * projected[..., 3 * channels :]
    ).astype(jnp.bfloat16)
    out_gate = jax.nn.sigmoid(
        jnp.dot(flat_cells, gate_weight, preferred_element_type=jnp.float32)
    ).reshape(row_count, col_count, channels)
    left_major = jnp.transpose(left_side, (2, 0, 1))
    right_major = jnp.transpose(right_side, (2, 0, 1))
    partial_sum = jnp.einsum(
        "cik,cjk->cij",
        left_major,
        lax.all_gather(right_major, "row", axis=1, tiled=True),
        preferred_element_type=jnp.float32,
    )
    summed = lax.psum_scatter(partial_sum, "col", scatter_dimension=2, tiled=True)
    normed_out = layer_norm(summed, out_gain[:, None, None], 0).astype(jnp.bfloat16)
    normed_cells = jnp.transpose(normed_out, (1, 2, 0))
    projected_out = jnp.dot(
        normed_cells.reshape(-1, channels), out_weight, preferred_element_type=jnp.float32
    ).reshape(row_count, col_count, channels)
    return (out_gate * projected_out).astype(jnp.bfloat16)


def kernel(x_ref, mask_ref, wp_ref, wg_ref, wo_ref, gin_ref, gout_ref, out_ref,
           normed, cells, mcol, rbuf, lbuf, lf32, acc, gate, nsend, nout,
           r_up, r_down, r_sib, r_recv, l_send, l_recv, n_send, n_recv):
    rows, keys, chan = x_ref.shape
    row = lax.axis_index("row")
    q = lax.axis_index("col")
    nz = lax.axis_size("row") // NY
    z, y = row // NY, row % NY
    sib = 1 - q
    ynb = z * NY + (1 - y)
    per_core = nz // 2
    home = z // per_core
    slot_own = jnp.where(q == home, z - per_core * q, per_core)
    piece = keys // PIECES

    barrier = pltpu.get_barrier_semaphore()

    def greet(r, c):
        pl.semaphore_signal(barrier, inc=1, device_id={"row": r, "col": c}, device_id_type=MESH)

    greet(row, sib)
    greet(ynb, q)

    @pl.when(z > 0)
    def _():
        greet(row - NY, q)

    @pl.when(z < nz - 1)
    def _():
        greet(row + NY, q)

    def r_copy(slot, half, p, to_row, to_col, sem, from_slot=None):
        where = pl.ds(pl.multiple_of(p * piece, piece), piece)
        src = slot if from_slot is None else from_slot
        return pltpu.make_async_remote_copy(
            src_ref=rbuf.at[src, half, where], dst_ref=rbuf.at[slot, half, where],
            send_sem=sem, recv_sem=r_recv.at[slot, half, p],
            device_id={"row": to_row, "col": to_col}, device_id_type=MESH)

    def up(slot, half, p):
        return r_copy(slot, half, p, row + NY, q, r_up.at[slot, half, p])

    def down(slot, half, p):
        return r_copy(slot, half, p, row - NY, q, r_down.at[slot, half, p])

    def to_sib(p):
        return r_copy(z - per_core * home, q, p, row, sib, r_sib.at[p], from_slot=per_core)

    def forward(slot, half, p, source, act):
        @pl.when((z >= source) & (z < nz - 1))
        def _():
            act(up(slot, half, p))

        @pl.when((z <= source) & (z > 0))
        def _():
            act(down(slot, half, p))

    def l_copy(i):
        src = (0, q) if i < 2 else (1, q)
        dst = (0, q) if i == 0 else (1, q)
        dev = {"row": ynb, "col": q} if i == 1 else {"row": row, "col": sib}
        return pltpu.make_async_remote_copy(
            src_ref=lbuf.at[src[0], src[1]], dst_ref=lbuf.at[dst[0], dst[1]],
            send_sem=l_send.at[i], recv_sem=l_recv.at[i], device_id=dev, device_id_type=MESH)

    def n_copy(rel):
        return pltpu.make_async_remote_copy(
            src_ref=nsend.at[rel], dst_ref=nout.at[rel * NY + y],
            send_sem=n_send.at[rel], recv_sem=n_recv.at[rel],
            device_id={"row": ynb, "col": q}, device_id_type=MESH)

    tokens = mask_ref.shape[1]
    mcol[...] = jnp.broadcast_to(mask_ref[...].astype(F32), (chan, tokens)).T
    mrow = mcol[pl.ds(pl.multiple_of(row * rows, rows), rows), :]

    def project(p, column):
        n = normed[:, p * piece:(p + 1) * piece, :].reshape(rows * piece, chan)
        both = jnp.dot(n, wp_ref[:, column:column + 2 * chan], preferred_element_type=F32)
        cells[...] = jax.nn.sigmoid(both[:, :chan]) * both[:, chan:]

    def masked(p, k):
        key = mcol[pl.ds(q * keys + p * piece + k, 1), :]
        return (cells[pl.ds(k, rows, stride=piece), :] * (mrow * key)).astype(BF16)

    def norm_rows(v, g):
        centre = jnp.mean(v, axis=-1, keepdims=True)
        shifted = v - centre
        spread = jnp.mean(shifted * shifted, axis=-1, keepdims=True)
        return (shifted * lax.rsqrt(spread + 1e-05) * g).astype(BF16)

    for p in range(PIECES):
        v = x_ref[:, p * piece:(p + 1) * piece, :].astype(F32).reshape(rows * piece, chan)
        normed[:, p * piece:(p + 1) * piece, :] = norm_rows(v, gin_ref[...]).reshape(rows, piece, chan)
        project(p, 2 * chan)

        def store_r(k, _):
            rbuf[slot_own, q, p * piece + k] = masked(p, k)
            return 0

        lax.fori_loop(0, piece, store_r, 0, unroll=8)
        if p == 0:
            pl.semaphore_wait(barrier, 2 + (z > 0).astype(jnp.int32) + (z < nz - 1).astype(jnp.int32))

        @pl.when(q == home)
        def _():
            forward(slot_own, q, p, z, lambda c: c.start())

        @pl.when(q != home)
        def _():
            to_sib(p).start()

    for p in range(PIECES):
        project(p, 0)

        def store_l(k, _):
            v = masked(p, k)
            lbuf[0, q, p * piece + k] = v
            lf32[0, q, p * piece + k] = v.astype(F32)
            return 0

        lax.fori_loop(0, piece, store_l, 0, unroll=8)
    l_copy(1).start()
    l_copy(0).start()

    for p in range(PIECES):
        n = normed[:, p * piece:(p + 1) * piece, :].reshape(rows * piece, chan)
        g = jax.nn.sigmoid(jnp.dot(n, wg_ref[...], preferred_element_type=F32))
        gate[:, p * piece:(p + 1) * piece, :] = g.reshape(rows, piece, chan)

    def widen(side, half):
        def step(k, _):
            lf32[side, half, k] = lbuf[side, half, k].astype(F32)
            return 0

        lax.fori_loop(0, keys, step, 0, unroll=8)

    l_copy(0).wait_recv()
    widen(0, sib)

    def combine(side, slot, half, start, count, first):
        def init(a):
            return jnp.where(first, 0.0, a)

        def step(k, sums):
            right = rbuf[slot, half, start + k].astype(F32)
            return tuple(
                sums[i] + lf32[side, half, start + k, pl.ds(i, HALF, stride=0), :][None] * right.reshape(2, 8, chan)
                for i in range(rows))

        sums = tuple(init(acc[side, i].reshape(2, 8, chan)) for i in range(rows))
        sums = lax.fori_loop(0, count, step, sums, unroll=4)
        for i in range(rows):
            acc[side, i] = sums[i].reshape(rows, chan)

    def finish(side, put):
        for b in range(0, rows, 8):
            v = acc[side, b:b + 8].reshape(8 * rows, chan)
            put(b, norm_rows(v, gout_ref[...]).reshape(8, rows, chan))

    near = jnp.clip(z - per_core * q, 0, per_core - 1)
    for t in range(2):
        slot = near if t == 0 else 1 - near
        source = per_core * q + slot

        def arrive(n, _):
            h, p = n // PIECES, n % PIECES
            half = jnp.where(h == 0, q, sib)

            @pl.when(jnp.logical_not((source == z) & (h == 0)))
            def _():
                up(slot, half, p).wait_recv()
                forward(slot, half, p, source, lambda c: c.start())

            combine(0, slot, half, p * piece, piece, n == 0)
            if t == 1:
                combine(1, slot, half, p * piece, piece, n == 0)
            return 0

        lax.fori_loop(0, 2 * PIECES, arrive, 0)
        if t == 0:
            l_copy(1).wait_recv()
            l_copy(2).start()
            widen(1, q)
            l_copy(2).wait_recv()
            widen(1, sib)
            combine(1, slot, q, 0, keys, True)
            combine(1, slot, sib, 0, keys, False)

        def put_send(b, v):
            nsend[slot, b:b + 8] = v

        def put_own(b, v):
            nout[slot * NY + y, b:b + 8] = v

        finish(1, put_send)
        n_copy(slot).start()
        finish(0, put_own)

    def emit(block, at):
        n = nout[block].reshape(rows * rows, chan)
        o = jnp.dot(n, wo_ref[...], preferred_element_type=F32).reshape(rows, rows, chan)
        where = pl.ds(pl.multiple_of(at * rows, rows), rows)
        out_ref[:, where, :] = (gate[:, where, :] * o).astype(BF16)

    for t in range(2):
        emit(t * NY + y, t * NY + y)
    for t in range(2):
        slot = near if t == 0 else 1 - near
        n_copy(slot).wait_recv()
        emit(slot * NY + 1 - y, slot * NY + 1 - y)

    for i in range(3):
        l_copy(i).wait_send()
    for t in range(2):
        n_copy(t).wait_send()

    def drain(n, _):
        slot, h, p = n // (2 * PIECES), (n // PIECES) % 2, n % PIECES
        forward(slot, h, p, per_core * q + slot, lambda c: c.wait_send())
        return 0

    lax.fori_loop(0, 4 * PIECES, drain, 0)

    @pl.when(q != home)
    def _():
        for p in range(PIECES):
            to_sib(p).wait_send()


def fused(pair_grid, token_mask, proj_weight, gate_weight, out_weight, in_gain, out_gain):
    rows, keys, chan = pair_grid.shape
    tokens = token_mask.shape[0]
    vmem = pl.BlockSpec(memory_space=pltpu.VMEM)
    dma = pltpu.SemaphoreType.DMA
    return pl.pallas_call(
        kernel,
        out_shape=jax.ShapeDtypeStruct(pair_grid.shape, BF16),
        in_specs=[vmem] * 7,
        out_specs=vmem,
        scratch_shapes=[
            pltpu.VMEM((rows, keys, chan), BF16),
            pltpu.VMEM((rows * keys // PIECES, chan), F32),
            pltpu.VMEM((tokens, chan), F32),
            pltpu.VMEM((3, 2, keys, rows, chan), BF16),
            pltpu.VMEM((2, 2, keys, rows, chan), BF16),
            pltpu.VMEM((2, 2, keys, rows, chan), F32),
            pltpu.VMEM((2, rows, rows, chan), F32),
            pltpu.VMEM((rows, keys, chan), F32),
            pltpu.VMEM((2, rows, rows, chan), BF16),
            pltpu.VMEM((4, rows, rows, chan), BF16),
            dma((2, 2, PIECES)),
            dma((2, 2, PIECES)),
            dma((PIECES,)),
            dma((2, 2, PIECES)),
            dma((3,)),
            dma((3,)),
            dma((2,)),
            dma((2,)),
        ],
        compiler_params=pltpu.CompilerParams(
            collective_id=0, has_side_effects=True, vmem_limit_bytes=40 * 1024 * 1024),
        cost_estimate=pl.CostEstimate(
            flops=4 * rows * keys * 2 * keys * chan, bytes_accessed=4 * rows * keys * chan, transcendentals=0),
    )(pair_grid, token_mask.reshape(1, tokens), proj_weight, gate_weight, out_weight,
      in_gain.reshape(1, chan), out_gain.reshape(1, chan))


def solution(mesh):
    placed = (P(("grp", "row"), "col", None), P("grp"), P(), P(), P(), P(), P())

    def run(pair_grid, *rest):
        rows, keys, chan = pair_grid.shape
        small = mesh.shape["row"] == 4 * NY and rows % 16 == 0 and keys == 4 * rows
        return (fused if small else body)(pair_grid, *rest)

    return jax.shard_map(
        run, mesh=mesh, in_specs=placed, out_specs=P(("grp", "row"), "col", None), check_vma=False
    )
```

```python
import jax
import jax.numpy as jnp
from jax import lax
from jax.experimental import pallas as pl
from jax.experimental.pallas import tpu as pltpu
from jax.sharding import PartitionSpec as P

MESH = pl.DeviceIdType.MESH
F32 = jnp.float32
BF16 = jnp.bfloat16
NY = 2
PIECES = 4
VMEM_BYTES = 63 * 1024 * 1024


def layer_norm(inputs, scales, along):
    centre = jnp.mean(inputs, axis=along, keepdims=True)
    shifted = inputs - centre
    spread = jnp.mean(shifted * shifted, axis=along, keepdims=True)
    return shifted * lax.rsqrt(spread + 1e-05) * scales


def body(pair_grid, token_mask, proj_weight, gate_weight, out_weight, in_gain, out_gain):
    row_count, col_count, channels = pair_grid.shape
    row_offset = lax.axis_index("row") * row_count
    col_offset = lax.axis_index("col") * col_count
    row_valid = lax.dynamic_slice_in_dim(token_mask, row_offset, row_count).astype(jnp.float32)
    col_valid = lax.dynamic_slice_in_dim(token_mask, col_offset, col_count).astype(jnp.float32)
    normed = layer_norm(pair_grid.astype(jnp.float32), in_gain, -1).astype(jnp.bfloat16)
    flat_cells = normed.reshape(-1, channels)
    projected = jnp.dot(flat_cells, proj_weight, preferred_element_type=jnp.float32).reshape(
        row_count, col_count, 4 * channels
    )
    pair_mask = (row_valid[:, None] * col_valid[None, :])[..., None]
    left_side = (
        pair_mask
        * jax.nn.sigmoid(projected[..., :channels])
        * projected[..., channels : 2 * channels]
    ).astype(jnp.bfloat16)
    right_side = (
        pair_mask
        * jax.nn.sigmoid(projected[..., 2 * channels : 3 * channels])
        * projected[..., 3 * channels :]
    ).astype(jnp.bfloat16)
    out_gate = jax.nn.sigmoid(
        jnp.dot(flat_cells, gate_weight, preferred_element_type=jnp.float32)
    ).reshape(row_count, col_count, channels)
    left_major = jnp.transpose(left_side, (2, 0, 1))
    right_major = jnp.transpose(right_side, (2, 0, 1))
    partial_sum = jnp.einsum(
        "cik,cjk->cij",
        left_major,
        lax.all_gather(right_major, "row", axis=1, tiled=True),
        preferred_element_type=jnp.float32,
    )
    summed = lax.psum_scatter(partial_sum, "col", scatter_dimension=2, tiled=True)
    normed_out = layer_norm(summed, out_gain[:, None, None], 0).astype(jnp.bfloat16)
    normed_cells = jnp.transpose(normed_out, (1, 2, 0))
    projected_out = jnp.dot(
        normed_cells.reshape(-1, channels), out_weight, preferred_element_type=jnp.float32
    ).reshape(row_count, col_count, channels)
    return (out_gate * projected_out).astype(jnp.bfloat16)


def kernel(x_hbm, mask_hbm, wp_hbm, wg_hbm, wo_hbm, gin_hbm, gout_hbm, out_ref,
           x_ref, mask_ref, wp_ref, wg_ref, wo_ref, gin_ref, gout_ref, load_sem,
           normed, cells, mcol, rbuf, lbuf, lf32, acc, gate, nsend, nout,
           r_up, r_down, r_sib, r_recv, l_send, l_recv, n_send, n_recv):
    rows, keys, chan = x_ref.shape
    row = lax.axis_index("row")
    q = lax.axis_index("col")
    nz = lax.axis_size("row") // NY
    z, y = row // NY, row % NY
    sib = 1 - q
    ynb = z * NY + (1 - y)
    per_core = nz // 2
    home = z // per_core
    slot_own = jnp.where(q == home, z - per_core * q, per_core)
    piece = keys // PIECES

    hbm = (mask_hbm, gin_hbm, x_hbm, wp_hbm, wg_hbm, wo_hbm, gout_hbm)
    local = (mask_ref, gin_ref, x_ref, wp_ref, wg_ref, wo_ref, gout_ref)
    loads = [pltpu.make_async_copy(a, b, load_sem.at[i]) for i, (a, b) in enumerate(zip(hbm, local))]
    for load in loads:
        load.start()

    barrier = pltpu.get_barrier_semaphore()

    def greet(r, c):
        pl.semaphore_signal(barrier, inc=1, device_id={"row": r, "col": c}, device_id_type=MESH)

    greet(row, sib)
    greet(ynb, q)

    @pl.when(z > 0)
    def _():
        greet(row - NY, q)

    @pl.when(z < nz - 1)
    def _():
        greet(row + NY, q)

    def r_copy(slot, half, p, to_row, to_col, sem, from_slot=None):
        where = pl.ds(pl.multiple_of(p * piece, piece), piece)
        src = slot if from_slot is None else from_slot
        return pltpu.make_async_remote_copy(
            src_ref=rbuf.at[src, half, where], dst_ref=rbuf.at[slot, half, where],
            send_sem=sem, recv_sem=r_recv.at[slot, half, p],
            device_id={"row": to_row, "col": to_col}, device_id_type=MESH)

    def up(slot, half, p):
        return r_copy(slot, half, p, row + NY, q, r_up.at[slot, half, p])

    def down(slot, half, p):
        return r_copy(slot, half, p, row - NY, q, r_down.at[slot, half, p])

    def to_sib(p):
        return r_copy(z - per_core * home, q, p, row, sib, r_sib.at[p], from_slot=per_core)

    def forward(slot, half, p, source, act):
        @pl.when((z >= source) & (z < nz - 1))
        def _():
            act(up(slot, half, p))

        @pl.when((z <= source) & (z > 0))
        def _():
            act(down(slot, half, p))

    def l_copy(i):
        src = (0, q) if i < 2 else (1, q)
        dst = (0, q) if i == 0 else (1, q)
        dev = {"row": ynb, "col": q} if i == 1 else {"row": row, "col": sib}
        return pltpu.make_async_remote_copy(
            src_ref=lbuf.at[src[0], src[1]], dst_ref=lbuf.at[dst[0], dst[1]],
            send_sem=l_send.at[i], recv_sem=l_recv.at[i], device_id=dev, device_id_type=MESH)

    def n_copy(rel):
        return pltpu.make_async_remote_copy(
            src_ref=nsend.at[rel], dst_ref=nout.at[rel * NY + y],
            send_sem=n_send.at[rel], recv_sem=n_recv.at[rel],
            device_id={"row": ynb, "col": q}, device_id_type=MESH)

    loads[0].wait()
    tokens = mask_ref.shape[1]
    mcol[...] = jnp.broadcast_to(mask_ref[...].astype(F32), (chan, tokens)).T
    mrow = mcol[pl.ds(pl.multiple_of(row * rows, rows), rows), :]

    def project(p, column):
        n = normed[:, p * piece:(p + 1) * piece, :].reshape(rows * piece, chan)
        both = jnp.dot(n, wp_ref[:, column:column + 2 * chan], preferred_element_type=F32)
        cells[...] = jax.nn.sigmoid(both[:, :chan]) * both[:, chan:]

    def masked(p, k):
        key = mcol[pl.ds(q * keys + p * piece + k, 1), :]
        return (cells[pl.ds(k, rows, stride=piece), :] * (mrow * key)).astype(BF16)

    def norm_rows(v, g):
        centre = jnp.mean(v, axis=-1, keepdims=True)
        shifted = v - centre
        spread = jnp.mean(shifted * shifted, axis=-1, keepdims=True)
        return (shifted * lax.rsqrt(spread + 1e-05) * g).astype(BF16)

    for load in loads[1:4]:
        load.wait()
    for p in range(PIECES):
        v = x_ref[:, p * piece:(p + 1) * piece, :].astype(F32).reshape(rows * piece, chan)
        normed[:, p * piece:(p + 1) * piece, :] = norm_rows(v, gin_ref[...]).reshape(rows, piece, chan)
        project(p, 2 * chan)

        def store_r(k, _):
            rbuf[slot_own, q, p * piece + k] = masked(p, k)
            return 0

        lax.fori_loop(0, piece, store_r, 0, unroll=8)
        if p == 0:
            pl.semaphore_wait(barrier, 2 + (z > 0).astype(jnp.int32) + (z < nz - 1).astype(jnp.int32))

        @pl.when(q == home)
        def _():
            forward(slot_own, q, p, z, lambda c: c.start())

        @pl.when(q != home)
        def _():
            to_sib(p).start()

    for p in range(PIECES):
        project(p, 0)

        def store_l(k, _):
            v = masked(p, k)
            lbuf[0, q, p * piece + k] = v
            lf32[0, q, p * piece + k] = v.astype(F32)
            return 0

        lax.fori_loop(0, piece, store_l, 0, unroll=8)
    l_copy(0).start()
    l_copy(1).start()

    def widen(side, half):
        def step(k, _):
            lf32[side, half, k] = lbuf[side, half, k].astype(F32)
            return 0

        lax.fori_loop(0, keys, step, 0, unroll=8)

    l_copy(0).wait_recv()
    widen(0, sib)

    def combine(side, slot, half, start, count, first):
        def init(a):
            return jnp.where(first, 0.0, a)

        def step(k, sums):
            right = rbuf[slot, half, start + k].astype(F32).reshape(2, 8, chan)
            return tuple(
                sums[i] + lf32[side, half, start + k, pl.ds(i, 8, stride=0), :][None] * right
                for i in range(rows))

        sums = tuple(init(acc[side, slot, i].reshape(2, 8, chan)) for i in range(rows))
        sums = lax.fori_loop(0, count, step, sums, unroll=4)
        for i in range(rows):
            acc[side, slot, i] = sums[i].reshape(rows, chan)

    def finish(side, slot, put):
        for b in range(0, rows, 8):
            v = acc[side, slot, b:b + 8].reshape(8 * rows, chan)
            put(b, norm_rows(v, gout_ref[...]).reshape(8, rows, chan))

    near = jnp.clip(z - per_core * q, 0, per_core - 1)
    far = 1 - near
    at_end = (z == 0) | (z == nz - 1)

    def arrive(slot, n, then):
        source = per_core * q + slot
        h, p = n // PIECES, n % PIECES
        half = jnp.where(h == 0, q, sib)

        @pl.when(jnp.logical_not((source == z) & (h == 0)))
        def _():
            up(slot, half, p).wait_recv()
            forward(slot, half, p, source, lambda c: c.start())

        combine(0, slot, half, p * piece, piece, n == 0)
        then(half, p)
        return 0

    def neighbour_left():
        l_copy(1).wait_recv()
        l_copy(2).start()
        widen(1, q)
        l_copy(2).wait_recv()
        widen(1, sib)

    def put_send(slot):
        def put(b, v):
            nsend[slot, b:b + 8] = v

        return put

    def put_own(slot):
        def put(b, v):
            nout[slot * NY + y, b:b + 8] = v

        return put

    def emit(block):
        n = nout[block].reshape(rows * rows, chan)
        o = jnp.dot(n, wo_ref[...], preferred_element_type=F32).reshape(rows, rows, chan)
        where = pl.ds(pl.multiple_of(block * rows, rows), rows)
        out_ref[:, where, :] = (gate[:, where, :] * o).astype(BF16)

    def close_neighbour(slot):
        finish(1, slot, put_send(slot))
        n_copy(slot).start()

    def close_own(slot):
        finish(0, slot, put_own(slot))
        emit(slot * NY + y)

    def close_other(slot):
        n_copy(slot).wait_recv()
        emit(slot * NY + 1 - y)

    lax.fori_loop(0, 2 * PIECES, lambda n, _: arrive(near, n, lambda half, p: None), 0)

    for load in loads[4:]:
        load.wait()
    for p in range(PIECES):
        n = normed[:, p * piece:(p + 1) * piece, :].reshape(rows * piece, chan)
        g = jax.nn.sigmoid(jnp.dot(n, wg_ref[...], preferred_element_type=F32))
        gate[:, p * piece:(p + 1) * piece, :] = g.reshape(rows, piece, chan)

    close_own(near)

    @pl.when(at_end)
    def _():
        neighbour_left()
        combine(1, near, q, 0, keys, True)
        combine(1, near, sib, 0, keys, False)
        close_neighbour(near)

    def second(n, _):
        def then(half, p):
            @pl.when(at_end)
            def _():
                combine(1, far, half, p * piece, piece, n == 0)

            @pl.when(jnp.logical_not(at_end) & (n >= PIECES))
            def _():
                combine(1, near, q, p * piece, piece, n == PIECES)
                combine(1, near, sib, p * piece, piece, False)
                combine(1, far, q, p * piece, piece, n == PIECES)
                combine(1, far, sib, p * piece, piece, False)

        pl.when(jnp.logical_not(at_end) & (n == PIECES))(neighbour_left)
        return arrive(far, n, then)

    lax.fori_loop(0, 2 * PIECES, second, 0)

    @pl.when(jnp.logical_not(at_end))
    def _():
        close_neighbour(near)

    close_neighbour(far)

    close_own(far)
    close_other(near)
    close_other(far)

    for i in range(3):
        l_copy(i).wait_send()
    for t in range(2):
        n_copy(t).wait_send()

    def drain(n, _):
        slot, h, p = n // (2 * PIECES), (n // PIECES) % 2, n % PIECES
        forward(slot, h, p, per_core * q + slot, lambda c: c.wait_send())
        return 0

    lax.fori_loop(0, 4 * PIECES, drain, 0)

    @pl.when(q != home)
    def _():
        for p in range(PIECES):
            to_sib(p).wait_send()


def fused(pair_grid, token_mask, proj_weight, gate_weight, out_weight, in_gain, out_gain):
    rows, keys, chan = pair_grid.shape
    tokens = token_mask.shape[0]
    vmem = pl.BlockSpec(memory_space=pltpu.VMEM)
    dma = pltpu.SemaphoreType.DMA
    operands = (pair_grid, token_mask.reshape(1, tokens), proj_weight, gate_weight, out_weight,
                in_gain.reshape(1, chan), out_gain.reshape(1, chan))
    return pl.pallas_call(
        kernel,
        out_shape=jax.ShapeDtypeStruct(pair_grid.shape, BF16),
        in_specs=[pl.BlockSpec(memory_space=pltpu.HBM)] * 7,
        out_specs=vmem,
        scratch_shapes=[
            *(pltpu.VMEM(a.shape, a.dtype) for a in operands),
            dma((7,)),
            pltpu.VMEM((rows, keys, chan), BF16),
            pltpu.VMEM((rows * keys // PIECES, chan), F32),
            pltpu.VMEM((tokens, chan), F32),
            pltpu.VMEM((3, 2, keys, rows, chan), BF16),
            pltpu.VMEM((2, 2, keys, rows, chan), BF16),
            pltpu.VMEM((2, 2, keys, rows, chan), F32),
            pltpu.VMEM((2, 2, rows, rows, chan), F32),
            pltpu.VMEM((rows, keys, chan), F32),
            pltpu.VMEM((2, rows, rows, chan), BF16),
            pltpu.VMEM((4, rows, rows, chan), BF16),
            dma((2, 2, PIECES)),
            dma((2, 2, PIECES)),
            dma((PIECES,)),
            dma((2, 2, PIECES)),
            dma((3,)),
            dma((3,)),
            dma((2,)),
            dma((2,)),
        ],
        compiler_params=pltpu.CompilerParams(
            collective_id=0, has_side_effects=True, vmem_limit_bytes=VMEM_BYTES),
        cost_estimate=pl.CostEstimate(
            flops=4 * rows * keys * 2 * keys * chan, bytes_accessed=4 * rows * keys * chan, transcendentals=0),
    )(*operands)


def solution(mesh):
    placed = (P(("grp", "row"), "col", None), P("grp"), P(), P(), P(), P(), P())

    def run(pair_grid, *rest):
        rows, keys, chan = pair_grid.shape
        small = mesh.shape["row"] == 4 * NY and rows % 16 == 0 and keys == 4 * rows
        return (fused if small else body)(pair_grid, *rest)

    return jax.shard_map(
        run, mesh=mesh, in_specs=placed, out_specs=P(("grp", "row"), "col", None), check_vma=False
    )
```

```python
import jax
import jax.numpy as jnp
from jax import lax
from jax.experimental import pallas as pl
from jax.experimental.pallas import tpu as pltpu
from jax.sharding import PartitionSpec as P

MESH = pl.DeviceIdType.MESH
F32 = jnp.float32
BF16 = jnp.bfloat16
NY = 2
PIECES = 4
VMEM_BYTES = 63 * 1024 * 1024


def layer_norm(inputs, scales, along):
    centre = jnp.mean(inputs, axis=along, keepdims=True)
    shifted = inputs - centre
    spread = jnp.mean(shifted * shifted, axis=along, keepdims=True)
    return shifted * lax.rsqrt(spread + 1e-05) * scales


def body(pair_grid, token_mask, proj_weight, gate_weight, out_weight, in_gain, out_gain):
    row_count, col_count, channels = pair_grid.shape
    row_offset = lax.axis_index("row") * row_count
    col_offset = lax.axis_index("col") * col_count
    row_valid = lax.dynamic_slice_in_dim(token_mask, row_offset, row_count).astype(jnp.float32)
    col_valid = lax.dynamic_slice_in_dim(token_mask, col_offset, col_count).astype(jnp.float32)
    normed = layer_norm(pair_grid.astype(jnp.float32), in_gain, -1).astype(jnp.bfloat16)
    flat_cells = normed.reshape(-1, channels)
    projected = jnp.dot(flat_cells, proj_weight, preferred_element_type=jnp.float32).reshape(
        row_count, col_count, 4 * channels
    )
    pair_mask = (row_valid[:, None] * col_valid[None, :])[..., None]
    left_side = (
        pair_mask
        * jax.nn.sigmoid(projected[..., :channels])
        * projected[..., channels : 2 * channels]
    ).astype(jnp.bfloat16)
    right_side = (
        pair_mask
        * jax.nn.sigmoid(projected[..., 2 * channels : 3 * channels])
        * projected[..., 3 * channels :]
    ).astype(jnp.bfloat16)
    out_gate = jax.nn.sigmoid(
        jnp.dot(flat_cells, gate_weight, preferred_element_type=jnp.float32)
    ).reshape(row_count, col_count, channels)
    left_major = jnp.transpose(left_side, (2, 0, 1))
    right_major = jnp.transpose(right_side, (2, 0, 1))
    partial_sum = jnp.einsum(
        "cik,cjk->cij",
        left_major,
        lax.all_gather(right_major, "row", axis=1, tiled=True),
        preferred_element_type=jnp.float32,
    )
    summed = lax.psum_scatter(partial_sum, "col", scatter_dimension=2, tiled=True)
    normed_out = layer_norm(summed, out_gain[:, None, None], 0).astype(jnp.bfloat16)
    normed_cells = jnp.transpose(normed_out, (1, 2, 0))
    projected_out = jnp.dot(
        normed_cells.reshape(-1, channels), out_weight, preferred_element_type=jnp.float32
    ).reshape(row_count, col_count, channels)
    return (out_gate * projected_out).astype(jnp.bfloat16)


def kernel(x_hbm, mask_hbm, wp_hbm, wg_hbm, wo_hbm, gin_hbm, gout_hbm, out_ref,
           x_ref, mask_ref, wp_ref, wg_ref, wo_ref, gin_ref, gout_ref, load_sem,
           normed, cells, mcol, rbuf, lbuf, lf32, acc, gate, nsend, nout,
           r_up, r_down, r_sib, r_recv, l_send, l_recv, n_send, n_recv):
    rows, keys, chan = x_ref.shape
    row = lax.axis_index("row")
    q = lax.axis_index("col")
    nz = lax.axis_size("row") // NY
    z, y = row // NY, row % NY
    sib = 1 - q
    ynb = z * NY + (1 - y)
    per_core = nz // 2
    home = z // per_core
    slot_own = jnp.where(q == home, z - per_core * q, per_core)
    piece = keys // PIECES

    hbm = (mask_hbm, gin_hbm, x_hbm, wp_hbm, wg_hbm, wo_hbm, gout_hbm)
    local = (mask_ref, gin_ref, x_ref, wp_ref, wg_ref, wo_ref, gout_ref)
    loads = [pltpu.make_async_copy(a, b, load_sem.at[i]) for i, (a, b) in enumerate(zip(hbm, local))]
    for load in loads:
        load.start()

    barrier = pltpu.get_barrier_semaphore()

    def greet(r, c):
        pl.semaphore_signal(barrier, inc=1, device_id={"row": r, "col": c}, device_id_type=MESH)

    greet(row, sib)
    greet(ynb, q)

    @pl.when(z > 0)
    def _():
        greet(row - NY, q)

    @pl.when(z < nz - 1)
    def _():
        greet(row + NY, q)

    def r_copy(slot, half, p, to_row, to_col, sem, from_slot=None):
        where = pl.ds(pl.multiple_of(p * piece, piece), piece)
        src = slot if from_slot is None else from_slot
        return pltpu.make_async_remote_copy(
            src_ref=rbuf.at[src, half, where], dst_ref=rbuf.at[slot, half, where],
            send_sem=sem, recv_sem=r_recv.at[slot, half, p],
            device_id={"row": to_row, "col": to_col}, device_id_type=MESH)

    def up(slot, half, p):
        return r_copy(slot, half, p, row + NY, q, r_up.at[slot, half, p])

    def down(slot, half, p):
        return r_copy(slot, half, p, row - NY, q, r_down.at[slot, half, p])

    def to_sib(p):
        return r_copy(z - per_core * home, q, p, row, sib, r_sib.at[p], from_slot=per_core)

    def forward(slot, half, p, source, act):
        @pl.when((z >= source) & (z < nz - 1))
        def _():
            act(up(slot, half, p))

        @pl.when((z <= source) & (z > 0))
        def _():
            act(down(slot, half, p))

    def l_copy(i):
        src = (0, q) if i < 2 else (1, q)
        dst = (0, q) if i == 0 else (1, q)
        dev = {"row": ynb, "col": q} if i == 1 else {"row": row, "col": sib}
        return pltpu.make_async_remote_copy(
            src_ref=lbuf.at[src[0], src[1]], dst_ref=lbuf.at[dst[0], dst[1]],
            send_sem=l_send.at[i], recv_sem=l_recv.at[i], device_id=dev, device_id_type=MESH)

    def n_copy(rel):
        return pltpu.make_async_remote_copy(
            src_ref=nsend.at[rel], dst_ref=nout.at[rel * NY + y],
            send_sem=n_send.at[rel], recv_sem=n_recv.at[rel],
            device_id={"row": ynb, "col": q}, device_id_type=MESH)

    loads[0].wait()
    tokens = mask_ref.shape[1]
    mcol[...] = jnp.broadcast_to(mask_ref[...].astype(F32), (chan, tokens)).T
    mrow = mcol[pl.ds(pl.multiple_of(row * rows, rows), rows), :]

    def project(p, column):
        n = normed[:, p * piece:(p + 1) * piece, :].reshape(rows * piece, chan)
        both = jnp.dot(n, wp_ref[:, column:column + 2 * chan], preferred_element_type=F32)
        cells[...] = jax.nn.sigmoid(both[:, :chan]) * both[:, chan:]

    def masked(p, k):
        key = mcol[pl.ds(q * keys + p * piece + k, 1), :]
        return (cells[pl.ds(k, rows, stride=piece), :] * (mrow * key)).astype(BF16)

    def norm_rows(v, g):
        centre = jnp.mean(v, axis=-1, keepdims=True)
        shifted = v - centre
        spread = jnp.mean(shifted * shifted, axis=-1, keepdims=True)
        return (shifted * lax.rsqrt(spread + 1e-05) * g).astype(BF16)

    for load in loads[1:4]:
        load.wait()
    for p in range(PIECES):
        v = x_ref[:, p * piece:(p + 1) * piece, :].astype(F32).reshape(rows * piece, chan)
        normed[:, p * piece:(p + 1) * piece, :] = norm_rows(v, gin_ref[...]).reshape(rows, piece, chan)
        project(p, 2 * chan)

        def store_r(k, _):
            rbuf[slot_own, q, p * piece + k] = masked(p, k)
            return 0

        lax.fori_loop(0, piece, store_r, 0, unroll=8)
        if p == 0:
            pl.semaphore_wait(barrier, 2 + (z > 0).astype(jnp.int32) + (z < nz - 1).astype(jnp.int32))

        @pl.when(q == home)
        def _():
            forward(slot_own, q, p, z, lambda c: c.start())

        @pl.when(q != home)
        def _():
            to_sib(p).start()

    for p in range(PIECES):
        project(p, 0)

        def store_l(k, _):
            v = masked(p, k)
            lbuf[0, q, p * piece + k] = v
            lf32[0, q, p * piece + k] = v.astype(F32)
            return 0

        lax.fori_loop(0, piece, store_l, 0, unroll=8)
    l_copy(0).start()
    l_copy(1).start()

    def widen(side, half):
        def step(k, _):
            lf32[side, half, k] = lbuf[side, half, k].astype(F32)
            return 0

        lax.fori_loop(0, keys, step, 0, unroll=8)

    def combine(side, slot, half, start, count, first):
        def init(a):
            return jnp.where(first, 0.0, a)

        def step(k, sums):
            right = rbuf[slot, half, start + k].astype(F32).reshape(2, 8, chan)
            return tuple(
                sums[i] + lf32[side, half, start + k, pl.ds(i, 8, stride=0), :][None] * right
                for i in range(rows))

        sums = tuple(init(acc[side, slot, i].reshape(2, 8, chan)) for i in range(rows))
        sums = lax.fori_loop(0, count, step, sums, unroll=4)
        for i in range(rows):
            acc[side, slot, i] = sums[i].reshape(rows, chan)

    def finish(side, slot, put):
        for b in range(0, rows, 8):
            v = acc[side, slot, b:b + 8].reshape(8 * rows, chan)
            put(b, norm_rows(v, gout_ref[...]).reshape(8, rows, chan))

    near = jnp.clip(z - per_core * q, 0, per_core - 1)
    far = 1 - near
    at_end = (z == 0) | (z == nz - 1)

    def arrive(slot, n, then):
        source = per_core * q + slot
        h, p = n // PIECES, n % PIECES
        half = jnp.where(h == 0, q, sib)

        @pl.when(jnp.logical_not((source == z) & (h == 0)))
        def _():
            up(slot, half, p).wait_recv()
            forward(slot, half, p, source, lambda c: c.start())

        then(half, p)
        return 0

    def pass_left():
        l_copy(1).wait_recv()
        l_copy(2).start()

    early = at_end & (q != home)

    def neighbour_left():
        pl.when(jnp.logical_not(early))(pass_left)
        widen(1, q)
        l_copy(2).wait_recv()
        widen(1, sib)

    def put_send(slot):
        def put(b, v):
            nsend[slot, b:b + 8] = v

        return put

    def put_own(slot):
        def put(b, v):
            nout[slot * NY + y, b:b + 8] = v

        return put

    def emit(block):
        n = nout[block].reshape(rows * rows, chan)
        o = jnp.dot(n, wo_ref[...], preferred_element_type=F32).reshape(rows, rows, chan)
        where = pl.ds(pl.multiple_of(block * rows, rows), rows)
        out_ref[:, where, :] = (gate[:, where, :] * o).astype(BF16)

    def close_neighbour(slot):
        finish(1, slot, put_send(slot))
        n_copy(slot).start()

    def close_own(slot):
        finish(0, slot, put_own(slot))
        emit(slot * NY + y)

    def close_other(slot):
        n_copy(slot).wait_recv()
        emit(slot * NY + 1 - y)

    pl.when(early)(pass_left)
    lax.fori_loop(0, 2 * PIECES, lambda n, _: arrive(near, n, lambda half, p: None), 0)

    l_copy(0).wait_recv()
    widen(0, sib)
    combine(0, near, q, 0, keys, True)
    combine(0, near, sib, 0, keys, False)

    def gate_and_near():
        for load in loads[4:]:
            load.wait()
        for p in range(PIECES):
            n = normed[:, p * piece:(p + 1) * piece, :].reshape(rows * piece, chan)
            g = jax.nn.sigmoid(jnp.dot(n, wg_ref[...], preferred_element_type=F32))
            gate[:, p * piece:(p + 1) * piece, :] = g.reshape(rows, piece, chan)

        close_own(near)

    @pl.when(at_end)
    def _():
        gate_and_near()
        neighbour_left()
        combine(1, near, q, 0, keys, True)
        combine(1, near, sib, 0, keys, False)
        close_neighbour(near)

    def second(n, _):
        def then(half, p):
            combine(0, far, half, p * piece, piece, n == 0)

            @pl.when(at_end)
            def _():
                combine(1, far, half, p * piece, piece, n == 0)

            @pl.when(jnp.logical_not(at_end) & (n >= PIECES))
            def _():
                combine(1, near, q, p * piece, piece, n == PIECES)
                combine(1, near, sib, p * piece, piece, False)
                combine(1, far, q, p * piece, piece, n == PIECES)
                combine(1, far, sib, p * piece, piece, False)

        @pl.when(jnp.logical_not(at_end) & (n == PIECES))
        def _():
            gate_and_near()
            neighbour_left()

        return arrive(far, n, then)

    lax.fori_loop(0, 2 * PIECES, second, 0)

    @pl.when(jnp.logical_not(at_end))
    def _():
        close_neighbour(near)

    close_neighbour(far)

    close_own(far)
    close_other(near)
    close_other(far)

    for i in range(3):
        l_copy(i).wait_send()
    for t in range(2):
        n_copy(t).wait_send()

    def drain(n, _):
        slot, h, p = n // (2 * PIECES), (n // PIECES) % 2, n % PIECES
        forward(slot, h, p, per_core * q + slot, lambda c: c.wait_send())
        return 0

    lax.fori_loop(0, 4 * PIECES, drain, 0)

    @pl.when(q != home)
    def _():
        for p in range(PIECES):
            to_sib(p).wait_send()


def fused(pair_grid, token_mask, proj_weight, gate_weight, out_weight, in_gain, out_gain):
    rows, keys, chan = pair_grid.shape
    tokens = token_mask.shape[0]
    vmem = pl.BlockSpec(memory_space=pltpu.VMEM)
    dma = pltpu.SemaphoreType.DMA
    operands = (pair_grid, token_mask.reshape(1, tokens), proj_weight, gate_weight, out_weight,
                in_gain.reshape(1, chan), out_gain.reshape(1, chan))
    return pl.pallas_call(
        kernel,
        out_shape=jax.ShapeDtypeStruct(pair_grid.shape, BF16),
        in_specs=[pl.BlockSpec(memory_space=pltpu.HBM)] * 7,
        out_specs=vmem,
        scratch_shapes=[
            *(pltpu.VMEM(a.shape, a.dtype) for a in operands),
            dma((7,)),
            pltpu.VMEM((rows, keys, chan), BF16),
            pltpu.VMEM((rows * keys // PIECES, chan), F32),
            pltpu.VMEM((tokens, chan), F32),
            pltpu.VMEM((3, 2, keys, rows, chan), BF16),
            pltpu.VMEM((2, 2, keys, rows, chan), BF16),
            pltpu.VMEM((2, 2, keys, rows, chan), F32),
            pltpu.VMEM((2, 2, rows, rows, chan), F32),
            pltpu.VMEM((rows, keys, chan), F32),
            pltpu.VMEM((2, rows, rows, chan), BF16),
            pltpu.VMEM((4, rows, rows, chan), BF16),
            dma((2, 2, PIECES)),
            dma((2, 2, PIECES)),
            dma((PIECES,)),
            dma((2, 2, PIECES)),
            dma((3,)),
            dma((3,)),
            dma((2,)),
            dma((2,)),
        ],
        compiler_params=pltpu.CompilerParams(
            collective_id=0, has_side_effects=True, vmem_limit_bytes=VMEM_BYTES),
        cost_estimate=pl.CostEstimate(
            flops=4 * rows * keys * 2 * keys * chan, bytes_accessed=4 * rows * keys * chan, transcendentals=0),
    )(*operands)


def solution(mesh):
    placed = (P(("grp", "row"), "col", None), P("grp"), P(), P(), P(), P(), P())

    def run(pair_grid, *rest):
        rows, keys, chan = pair_grid.shape
        small = mesh.shape["row"] == 4 * NY and rows % 16 == 0 and keys == 4 * rows
        return (fused if small else body)(pair_grid, *rest)

    return jax.shard_map(
        run, mesh=mesh, in_specs=placed, out_specs=P(("grp", "row"), "col", None), check_vma=False
    )
```

```python
import jax
import jax.numpy as jnp
from jax import lax
from jax.experimental import pallas as pl
from jax.experimental.pallas import tpu as pltpu
from jax.sharding import PartitionSpec as P

MESH = pl.DeviceIdType.MESH
F32 = jnp.float32
BF16 = jnp.bfloat16
NY = 2
PIECES = 4
VMEM_BYTES = 63 * 1024 * 1024


def layer_norm(inputs, scales, along):
    centre = jnp.mean(inputs, axis=along, keepdims=True)
    shifted = inputs - centre
    spread = jnp.mean(shifted * shifted, axis=along, keepdims=True)
    return shifted * lax.rsqrt(spread + 1e-05) * scales


def body(pair_grid, token_mask, proj_weight, gate_weight, out_weight, in_gain, out_gain):
    row_count, col_count, channels = pair_grid.shape
    row_offset = lax.axis_index("row") * row_count
    col_offset = lax.axis_index("col") * col_count
    row_valid = lax.dynamic_slice_in_dim(token_mask, row_offset, row_count).astype(jnp.float32)
    col_valid = lax.dynamic_slice_in_dim(token_mask, col_offset, col_count).astype(jnp.float32)
    normed = layer_norm(pair_grid.astype(jnp.float32), in_gain, -1).astype(jnp.bfloat16)
    flat_cells = normed.reshape(-1, channels)
    projected = jnp.dot(flat_cells, proj_weight, preferred_element_type=jnp.float32).reshape(
        row_count, col_count, 4 * channels
    )
    pair_mask = (row_valid[:, None] * col_valid[None, :])[..., None]
    left_side = (
        pair_mask
        * jax.nn.sigmoid(projected[..., :channels])
        * projected[..., channels : 2 * channels]
    ).astype(jnp.bfloat16)
    right_side = (
        pair_mask
        * jax.nn.sigmoid(projected[..., 2 * channels : 3 * channels])
        * projected[..., 3 * channels :]
    ).astype(jnp.bfloat16)
    out_gate = jax.nn.sigmoid(
        jnp.dot(flat_cells, gate_weight, preferred_element_type=jnp.float32)
    ).reshape(row_count, col_count, channels)
    left_major = jnp.transpose(left_side, (2, 0, 1))
    right_major = jnp.transpose(right_side, (2, 0, 1))
    partial_sum = jnp.einsum(
        "cik,cjk->cij",
        left_major,
        lax.all_gather(right_major, "row", axis=1, tiled=True),
        preferred_element_type=jnp.float32,
    )
    summed = lax.psum_scatter(partial_sum, "col", scatter_dimension=2, tiled=True)
    normed_out = layer_norm(summed, out_gain[:, None, None], 0).astype(jnp.bfloat16)
    normed_cells = jnp.transpose(normed_out, (1, 2, 0))
    projected_out = jnp.dot(
        normed_cells.reshape(-1, channels), out_weight, preferred_element_type=jnp.float32
    ).reshape(row_count, col_count, channels)
    return (out_gate * projected_out).astype(jnp.bfloat16)


def kernel(x_hbm, mask_hbm, wp_hbm, wg_hbm, wo_hbm, gin_hbm, gout_hbm, out_ref,
           x_ref, mask_ref, wp_ref, wg_ref, wo_ref, gin_ref, gout_ref, load_sem,
           normed, cells, mcol, rbuf, lbuf, lf32, acc, gate, nsend, nout,
           r_up, r_down, r_sib, r_recv, l_send, l_recv, n_send, n_recv):
    rows, keys, chan = x_ref.shape
    row = lax.axis_index("row")
    q = lax.axis_index("col")
    nz = lax.axis_size("row") // NY
    z, y = row // NY, row % NY
    sib = 1 - q
    ynb = z * NY + (1 - y)
    per_core = nz // 2
    home = z // per_core
    slot_own = jnp.where(q == home, z - per_core * q, per_core)
    piece = keys // PIECES

    hbm = (mask_hbm, gin_hbm, x_hbm, wp_hbm, wg_hbm, wo_hbm, gout_hbm)
    local = (mask_ref, gin_ref, x_ref, wp_ref, wg_ref, wo_ref, gout_ref)
    loads = [pltpu.make_async_copy(a, b, load_sem.at[i]) for i, (a, b) in enumerate(zip(hbm, local))]
    for load in loads:
        load.start()

    barrier = pltpu.get_barrier_semaphore()

    def greet(r, c):
        pl.semaphore_signal(barrier, inc=1, device_id={"row": r, "col": c}, device_id_type=MESH)

    greet(row, sib)
    greet(ynb, q)

    @pl.when(z > 0)
    def _():
        greet(row - NY, q)

    @pl.when(z < nz - 1)
    def _():
        greet(row + NY, q)

    def r_copy(slot, half, p, to_row, to_col, sem, from_slot=None):
        where = pl.ds(pl.multiple_of(p * piece, piece), piece)
        src = slot if from_slot is None else from_slot
        return pltpu.make_async_remote_copy(
            src_ref=rbuf.at[src, half, where], dst_ref=rbuf.at[slot, half, where],
            send_sem=sem, recv_sem=r_recv.at[slot, half, p],
            device_id={"row": to_row, "col": to_col}, device_id_type=MESH)

    def up(slot, half, p):
        return r_copy(slot, half, p, row + NY, q, r_up.at[slot, half, p])

    def down(slot, half, p):
        return r_copy(slot, half, p, row - NY, q, r_down.at[slot, half, p])

    def to_sib(p):
        return r_copy(z - per_core * home, q, p, row, sib, r_sib.at[p], from_slot=per_core)

    def forward(slot, half, p, source, act):
        @pl.when((z >= source) & (z < nz - 1))
        def _():
            act(up(slot, half, p))

        @pl.when((z <= source) & (z > 0))
        def _():
            act(down(slot, half, p))

    def l_copy(i):
        src = (0, q) if i < 2 else (1, q)
        dst = (0, q) if i == 0 else (1, q)
        dev = {"row": ynb, "col": q} if i == 1 else {"row": row, "col": sib}
        return pltpu.make_async_remote_copy(
            src_ref=lbuf.at[src[0], src[1]], dst_ref=lbuf.at[dst[0], dst[1]],
            send_sem=l_send.at[i], recv_sem=l_recv.at[i], device_id=dev, device_id_type=MESH)

    def n_copy(rel):
        return pltpu.make_async_remote_copy(
            src_ref=nsend.at[rel], dst_ref=nout.at[rel * NY + y],
            send_sem=n_send.at[rel], recv_sem=n_recv.at[rel],
            device_id={"row": ynb, "col": q}, device_id_type=MESH)

    loads[0].wait()
    tokens = mask_ref.shape[1]
    mcol[...] = jnp.broadcast_to(mask_ref[...].astype(F32), (chan, tokens)).T
    mrow = mcol[pl.ds(pl.multiple_of(row * rows, rows), rows), :]

    def project(p, column):
        n = normed[:, p * piece:(p + 1) * piece, :].reshape(rows * piece, chan)
        both = jnp.dot(n, wp_ref[:, column:column + 2 * chan], preferred_element_type=F32)
        cells[...] = jax.nn.sigmoid(both[:, :chan]) * both[:, chan:]

    def masked(p, k):
        key = mcol[pl.ds(q * keys + p * piece + k, 1), :]
        return (cells[pl.ds(k, rows, stride=piece), :] * (mrow * key)).astype(BF16)

    def norm_rows(v, g):
        centre = jnp.mean(v, axis=-1, keepdims=True)
        shifted = v - centre
        spread = jnp.mean(shifted * shifted, axis=-1, keepdims=True)
        return (shifted * lax.rsqrt(spread + 1e-05) * g).astype(BF16)

    for load in loads[1:4]:
        load.wait()
    for p in range(PIECES):
        v = x_ref[:, p * piece:(p + 1) * piece, :].astype(F32).reshape(rows * piece, chan)
        normed[:, p * piece:(p + 1) * piece, :] = norm_rows(v, gin_ref[...]).reshape(rows, piece, chan)
        project(p, 2 * chan)

        def store_r(k, _):
            rbuf[slot_own, q, p * piece + k] = masked(p, k)
            return 0

        lax.fori_loop(0, piece, store_r, 0, unroll=8)
        if p == 0:
            pl.semaphore_wait(barrier, 2 + (z > 0).astype(jnp.int32) + (z < nz - 1).astype(jnp.int32))

        @pl.when(q == home)
        def _():
            forward(slot_own, q, p, z, lambda c: c.start())

        @pl.when(q != home)
        def _():
            to_sib(p).start()

    for p in range(PIECES):
        project(p, 0)

        def store_l(k, _):
            v = masked(p, k)
            lbuf[0, q, p * piece + k] = v
            lf32[0, q, p * piece + k] = v.astype(F32)
            return 0

        lax.fori_loop(0, piece, store_l, 0, unroll=8)
    l_copy(0).start()
    l_copy(1).start()

    def widen(side, half):
        def step(k, _):
            lf32[side, half, k] = lbuf[side, half, k].astype(F32)
            return 0

        lax.fori_loop(0, keys, step, 0, unroll=8)

    def combine(side, slot, half, start, count, first):
        def init(a):
            return jnp.where(first, 0.0, a)

        def step(k, sums):
            right = rbuf[slot, half, start + k].astype(F32).reshape(2, 8, chan)
            return tuple(
                sums[i] + lf32[side, half, start + k, pl.ds(i, 8, stride=0), :][None] * right
                for i in range(rows))

        sums = tuple(init(acc[side, slot, i].reshape(2, 8, chan)) for i in range(rows))
        sums = lax.fori_loop(0, count, step, sums, unroll=4)
        for i in range(rows):
            acc[side, slot, i] = sums[i].reshape(rows, chan)

    def finish(side, slot, put):
        for b in range(0, rows, 8):
            v = acc[side, slot, b:b + 8].reshape(8 * rows, chan)
            put(b, norm_rows(v, gout_ref[...]).reshape(8, rows, chan))

    near = jnp.clip(z - per_core * q, 0, per_core - 1)
    far = 1 - near
    at_end = (z == 0) | (z == nz - 1)

    def arrive(slot, n, then):
        source = per_core * q + slot
        h, p = n // PIECES, n % PIECES
        half = jnp.where(h == 0, q, sib)

        @pl.when(jnp.logical_not((source == z) & (h == 0)))
        def _():
            up(slot, half, p).wait_recv()
            forward(slot, half, p, source, lambda c: c.start())

        then(half, p)
        return 0

    def pass_left():
        l_copy(1).wait_recv()
        l_copy(2).start()

    early = at_end & (q != home)

    def neighbour_left():
        pl.when(jnp.logical_not(early))(pass_left)
        widen(1, q)
        l_copy(2).wait_recv()
        widen(1, sib)

    def put_send(slot):
        def put(b, v):
            nsend[slot, b:b + 8] = v

        return put

    def put_own(slot):
        def put(b, v):
            nout[slot * NY + y, b:b + 8] = v

        return put

    def emit(block):
        n = nout[block].reshape(rows * rows, chan)
        o = jnp.dot(n, wo_ref[...], preferred_element_type=F32).reshape(rows, rows, chan)
        where = pl.ds(pl.multiple_of(block * rows, rows), rows)
        out_ref[:, where, :] = (gate[:, where, :] * o).astype(BF16)

    def close_neighbour(slot):
        finish(1, slot, put_send(slot))
        n_copy(slot).start()

    def close_own(slot):
        finish(0, slot, put_own(slot))
        emit(slot * NY + y)

    def close_other(slot):
        n_copy(slot).wait_recv()
        emit(slot * NY + 1 - y)

    pl.when(early)(pass_left)
    lax.fori_loop(0, 2 * PIECES, lambda n, _: arrive(near, n, lambda half, p: None), 0)

    l_copy(0).wait_recv()
    widen(0, sib)
    combine(0, near, q, 0, keys, True)
    combine(0, near, sib, 0, keys, False)

    def gate_and_near():
        for load in loads[4:]:
            load.wait()
        for p in range(PIECES):
            n = normed[:, p * piece:(p + 1) * piece, :].reshape(rows * piece, chan)
            g = jax.nn.sigmoid(jnp.dot(n, wg_ref[...], preferred_element_type=F32))
            gate[:, p * piece:(p + 1) * piece, :] = g.reshape(rows, piece, chan)

        close_own(near)

    ahead = at_end | (q != home)

    @pl.when(ahead)
    def _():
        gate_and_near()
        neighbour_left()
        combine(1, near, q, 0, keys, True)
        combine(1, near, sib, 0, keys, False)
        close_neighbour(near)

    def second(n, _):
        def then(half, p):
            combine(0, far, half, p * piece, piece, n == 0)

            @pl.when(ahead)
            def _():
                combine(1, far, half, p * piece, piece, n == 0)

        return arrive(far, n, then)

    lax.fori_loop(0, 2 * PIECES, second, 0)

    @pl.when(jnp.logical_not(ahead))
    def _():
        gate_and_near()
        neighbour_left()
        for slot in (near, far):
            combine(1, slot, q, 0, keys, True)
            combine(1, slot, sib, 0, keys, False)
        close_neighbour(near)

    close_neighbour(far)

    close_own(far)
    close_other(near)
    close_other(far)

    for i in range(3):
        l_copy(i).wait_send()
    for t in range(2):
        n_copy(t).wait_send()

    def drain(n, _):
        slot, h, p = n // (2 * PIECES), (n // PIECES) % 2, n % PIECES
        forward(slot, h, p, per_core * q + slot, lambda c: c.wait_send())
        return 0

    lax.fori_loop(0, 4 * PIECES, drain, 0)

    @pl.when(q != home)
    def _():
        for p in range(PIECES):
            to_sib(p).wait_send()


def fused(pair_grid, token_mask, proj_weight, gate_weight, out_weight, in_gain, out_gain):
    rows, keys, chan = pair_grid.shape
    tokens = token_mask.shape[0]
    vmem = pl.BlockSpec(memory_space=pltpu.VMEM)
    dma = pltpu.SemaphoreType.DMA
    operands = (pair_grid, token_mask.reshape(1, tokens), proj_weight, gate_weight, out_weight,
                in_gain.reshape(1, chan), out_gain.reshape(1, chan))
    return pl.pallas_call(
        kernel,
        out_shape=jax.ShapeDtypeStruct(pair_grid.shape, BF16),
        in_specs=[pl.BlockSpec(memory_space=pltpu.HBM)] * 7,
        out_specs=vmem,
        scratch_shapes=[
            *(pltpu.VMEM(a.shape, a.dtype) for a in operands),
            dma((7,)),
            pltpu.VMEM((rows, keys, chan), BF16),
            pltpu.VMEM((rows * keys // PIECES, chan), F32),
            pltpu.VMEM((tokens, chan), F32),
            pltpu.VMEM((3, 2, keys, rows, chan), BF16),
            pltpu.VMEM((2, 2, keys, rows, chan), BF16),
            pltpu.VMEM((2, 2, keys, rows, chan), F32),
            pltpu.VMEM((2, 2, rows, rows, chan), F32),
            pltpu.VMEM((rows, keys, chan), F32),
            pltpu.VMEM((2, rows, rows, chan), BF16),
            pltpu.VMEM((4, rows, rows, chan), BF16),
            dma((2, 2, PIECES)),
            dma((2, 2, PIECES)),
            dma((PIECES,)),
            dma((2, 2, PIECES)),
            dma((3,)),
            dma((3,)),
            dma((2,)),
            dma((2,)),
        ],
        compiler_params=pltpu.CompilerParams(
            collective_id=0, has_side_effects=True, vmem_limit_bytes=VMEM_BYTES),
        cost_estimate=pl.CostEstimate(
            flops=4 * rows * keys * 2 * keys * chan, bytes_accessed=4 * rows * keys * chan, transcendentals=0),
    )(*operands)


def solution(mesh):
    placed = (P(("grp", "row"), "col", None), P("grp"), P(), P(), P(), P(), P())

    def run(pair_grid, *rest):
        rows, keys, chan = pair_grid.shape
        small = mesh.shape["row"] == 4 * NY and rows % 16 == 0 and keys == 4 * rows
        return (fused if small else body)(pair_grid, *rest)

    return jax.shard_map(
        run, mesh=mesh, in_specs=placed, out_specs=P(("grp", "row"), "col", None), check_vma=False
    )
```
